32 devices in a mesh: dp: 8 (over y, x, core), seq: 4 (over z).
Axes of the slice: x: 2, y: 2, z: 4, core: 2. Of those that a mesh axis runs over, the one named last changes fastest.
Arguments:
- query_rows: bfloat16 [4096, 4096], P(('dp', 'seq')), parts along dimension 0, may hold values from -32 to 32
- key_rows: bfloat16 [4096, 4096], P(('dp', 'seq')), parts along dimension 0, may hold values from -32 to 32
- value_rows: bfloat16 [4096, 4096], P(('dp', 'seq')), parts along dimension 0, may hold values from -6 to 6
- query_tangent: bfloat16 [4096, 4096], P(('dp', 'seq')), parts along dimension 0, may hold values from -6 to 6
- key_tangent: bfloat16 [4096, 4096], P(('dp', 'seq')), parts along dimension 0, may hold values from -6 to 6
- value_tangent: bfloat16 [4096, 4096], P(('dp', 'seq')), parts along dimension 0, may hold values from -6 to 6
Outputs:
- attended: bfloat16 [4096, 4096], P(('dp', 'seq')), parts along dimension 0
- attended_tangent: bfloat16 [4096, 4096], P(('dp', 'seq')), parts along dimension 0
The draws below stay inside these ranges and needn't reach their ends.
There are 8 independent parts, one for each index of `dp`. The reference program is written for one: setup_inputs(seed, part) draws one part's arguments, and reference() takes and returns one part's arrays. A program takes and returns all parts, laid end to end along the dimension named above; each array names one. Nothing has to cross between parts.
All inputs are finite; a program needn't handle non-finite values.
Results may differ from the reference program's by a relative error of at most 0.0049.
Values may be sent and summed in bfloat16 or wider, within the bound.
No kernel may reach another device: no remote copies, remote signals or barrier semaphores. Data moves between devices by JAX's collectives and lax.ppermute only.
A program may use at most 64 MiB of HBM per device.

```python
import jax
import jax.numpy as jnp
from jax import lax

HEADS = 32
HEAD = 128
TOKENS = 512


def draw_query_rows(key, part):
    fresh_key = jax.random.fold_in(key, 11)
    sample = jnp.clip(1.4 * jax.random.normal(fresh_key, (TOKENS, HEADS, HEAD), jnp.float32), -8.0, 8.0)
    return sample.reshape(TOKENS, HEADS * HEAD).astype(jnp.bfloat16)


def draw_key_rows(key, part):
    fresh_key = jax.random.fold_in(key, 13)
    sample = jnp.clip(1.4 * jax.random.normal(fresh_key, (TOKENS, HEADS, HEAD), jnp.float32), -8.0, 8.0)
    return sample.reshape(TOKENS, HEADS * HEAD).astype(jnp.bfloat16)


def level_of(rng, shape, cuts, low, top_value):
    def one(position, parts):
        steps = jax.random.uniform(jax.random.fold_in(jax.random.fold_in(rng, 6), position), (parts,), jnp.float32, low / len(cuts), top_value / len(cuts))
        return jnp.repeat(jnp.exp(steps), shape[position] // parts).reshape((-1,) + (1,) * (len(shape) - position - 1))

    loudness = one(*cuts[0])
    for cut in cuts[1:]:
        loudness = loudness * one(*cut)
    return loudness


def bell_draw(rng, shape, width, most, cuts=(), kind=jnp.bfloat16):
    level = level_of(rng, shape, cuts, -0.22, 0.18) if cuts else 1.0
    array = jax.random.normal(rng, shape, jnp.float32) * width * level
    return jnp.minimum(jnp.maximum(array, -most), most).astype(kind)


def setup_inputs(seed: int = 0, part: int = 0) -> dict:
    streams_of = jax.random.split(jax.random.key(seed), 7)
    part_keys = jax.random.split(jax.random.fold_in(streams_of[6], part), 7)
    return {
        "query_rows": draw_query_rows(jax.random.fold_in(jax.random.fold_in(streams_of[6], part), 71), part),
        "key_rows": draw_key_rows(jax.random.fold_in(jax.random.fold_in(streams_of[6], part), 71), part),
        "value_rows": bell_draw(part_keys[2], (TOKENS, HEADS * HEAD), 1.0, 6.0, ((0, 4),)),
        "query_tangent": bell_draw(part_keys[3], (TOKENS, HEADS * HEAD), 1.0, 6.0, ((0, 4),)),
        "key_tangent": bell_draw(part_keys[4], (TOKENS, HEADS * HEAD), 1.0, 6.0, ((0, 4),)),
        "value_tangent": bell_draw(part_keys[5], (TOKENS, HEADS * HEAD), 1.0, 6.0, ((0, 4),)),
    }


def one_head(pieces):
    head_queries, head_keys, head_values, query_tangent, key_tangent, value_tangent = pieces
    score_scale = HEAD ** -0.5
    scores = jnp.dot(head_queries, head_keys.T, preferred_element_type=jnp.float32) * score_scale
    score_tangent = (jnp.dot(query_tangent, head_keys.T, preferred_element_type=jnp.float32)
                     + jnp.dot(head_queries, key_tangent.T, preferred_element_type=jnp.float32)) * score_scale
    row_max = jnp.max(scores, axis=1, keepdims=True)
    raised = jnp.exp(scores - row_max)
    exact_weights = raised / jnp.sum(raised, axis=1, keepdims=True)
    weights = exact_weights.astype(jnp.bfloat16)
    output = jnp.dot(weights, head_values, preferred_element_type=jnp.float32).astype(jnp.bfloat16)
    mean_tangent = jnp.sum(exact_weights * score_tangent, axis=1, keepdims=True)
    weight_tangent = (exact_weights * (score_tangent - mean_tangent)).astype(jnp.bfloat16)
    tangent = (jnp.dot(weight_tangent, head_values, preferred_element_type=jnp.float32)
               + jnp.dot(weights, value_tangent, preferred_element_type=jnp.float32)).astype(jnp.bfloat16)
    return output, tangent


def by_heads(matrix):
    return matrix.reshape(TOKENS, HEADS, HEAD).transpose(1, 0, 2)


def reference(query_rows, key_rows, value_rows, query_tangent, key_tangent, value_tangent):
    outputs, tangents = lax.map(one_head, (by_heads(query_rows), by_heads(key_rows), by_heads(value_rows),
                                           by_heads(query_tangent), by_heads(key_tangent), by_heads(value_tangent)))
    attended = outputs.transpose(1, 0, 2).reshape(TOKENS, HEADS * HEAD)
    attended_tangent = tangents.transpose(1, 0, 2).reshape(TOKENS, HEADS * HEAD)
    return attended, attended_tangent
```

```python
import functools
import math

import jax
import jax.numpy as jnp
from jax import lax
from jax.experimental import pallas as pl
from jax.experimental.pallas import tpu as pltpu
from jax.sharding import PartitionSpec as P

HEADS = 32
HEAD = 128
ANYWHERE = pl.BlockSpec(memory_space=pl.ANY)


def chunk_sizes(count):
    sizes = []
    while count > 2:
        sizes.append(count // 2)
        count -= count // 2
    return sizes + [count]


def rounds_of(count):
    if count & (count - 1) == 0:
        return [[i ^ step for i in range(count)] for step in range(count - 1, 0, -1)]
    return [[(i + step) % count for i in range(count)] for step in range(1, count)]


def columns(start, width):
    return pl.ds(pl.multiple_of(start, HEAD), width)


def pack_kernel(count, width, starts, *refs):
    arrays, messages, sems = refs[:6], refs[6:6 + count], refs[6 + count]
    copies = []
    for m in range(count):
        for i in range(6):
            copies.append(
                pltpu.make_async_copy(
                    arrays[i].at[:, columns(starts[m], width)], messages[m].at[i], sems.at[m, i]
                )
            )
    for copy in copies:
        copy.start()
    for copy in copies:
        copy.wait()


def pack(arrays, starts, width):
    count = len(starts)
    rows = arrays[0].shape[0]
    message = jax.ShapeDtypeStruct((6, rows, width), arrays[0].dtype)
    return pl.pallas_call(
        functools.partial(pack_kernel, count, width),
        out_shape=[message] * count,
        in_specs=[pl.BlockSpec(memory_space=pltpu.SMEM)] + [ANYWHERE] * 6,
        out_specs=[ANYWHERE] * count,
        scratch_shapes=[pltpu.SemaphoreType.DMA((count, 6))],
        cost_estimate=pl.CostEstimate(
            flops=0, bytes_accessed=count * 6 * rows * width * 4, transcendentals=0
        ),
        name="pack",
    )(jnp.stack(starts).astype(jnp.int32), *arrays)


def place_kernel(count, width, starts, *refs):
    messages = refs[:count]
    outs = refs[-3:-1]
    sems = refs[-1]
    copies = []
    for m in range(count):
        for i in range(2):
            copies.append(
                pltpu.make_async_copy(
                    messages[m].at[i], outs[i].at[:, columns(starts[m], width)], sems.at[m, i]
                )
            )
    for copy in copies:
        copy.start()
    for copy in copies:
        copy.wait()


def place(outs, messages, starts, shape):
    count = len(messages)
    _, rows, width = messages[0].shape
    out = jax.ShapeDtypeStruct(shape, messages[0].dtype)
    return pl.pallas_call(
        functools.partial(place_kernel, count, width),
        out_shape=[out, out],
        in_specs=[pl.BlockSpec(memory_space=pltpu.SMEM)] + [ANYWHERE] * (count + len(outs)),
        out_specs=[ANYWHERE, ANYWHERE],
        scratch_shapes=[pltpu.SemaphoreType.DMA((count, 2))],
        input_output_aliases={1 + count + i: i for i in range(len(outs))},
        cost_estimate=pl.CostEstimate(
            flops=0, bytes_accessed=count * rows * width * 8, transcendentals=0
        ),
        name="place",
    )(jnp.stack(starts).astype(jnp.int32), *messages, *outs)


def attend_kernel(groups, start, *refs):
    own, messages = refs[:6], refs[6:6 + groups - 1]
    results = refs[6 + groups - 1:]
    del start

    def piece(which, group):
        return own[which][...] if group == 0 else messages[group - 1][which]

    def joined(which):
        return jnp.concatenate([piece(which, g) for g in range(groups)], axis=0)

    keys = joined(1)
    values = joined(2)
    both_keys = jnp.concatenate([keys, joined(4)], axis=1)
    both_values = jnp.concatenate([values, joined(5)], axis=1)
    width = keys.shape[1]
    scale = width ** -0.5
    across = (((1,), (1,)), ((), ()))
    for g in range(groups):
        queries = piece(0, g)
        paired = jnp.concatenate([piece(3, g), queries], axis=1)
        scores = lax.dot_general(queries, keys, across, preferred_element_type=jnp.float32)
        tangent = lax.dot_general(paired, both_keys, across, preferred_element_type=jnp.float32)
        row_max = jnp.max(scores, axis=1, keepdims=True)
        raised = jnp.exp2((scores - row_max) * (scale * math.log2(math.e)))
        exact = raised * (1.0 / jnp.sum(raised, axis=1, keepdims=True))
        weights = exact.astype(jnp.bfloat16)
        mean = jnp.sum(exact * tangent, axis=1, keepdims=True)
        weight_tangent = (exact * ((tangent - mean) * scale)).astype(jnp.bfloat16)
        sums = jnp.dot(weights, both_values, preferred_element_type=jnp.float32)
        moved = jnp.dot(weight_tangent, values, preferred_element_type=jnp.float32)
        results[g][0] = sums[:, :width].astype(jnp.bfloat16)
        results[g][1] = (sums[:, width:] + moved).astype(jnp.bfloat16)


def attend(arrays, messages, start, heads):
    groups = len(messages) + 1
    rows = arrays[0].shape[0]
    tokens = rows * groups
    own = pl.BlockSpec((rows, HEAD), lambda h, s: (0, s[0] + h))
    message = pl.BlockSpec((6, rows, HEAD), lambda h, s: (0, 0, h))
    result = pl.BlockSpec((2, rows, HEAD), lambda h, s: (0, 0, h))
    return pl.pallas_call(
        functools.partial(attend_kernel, groups),
        out_shape=[jax.ShapeDtypeStruct((2, rows, heads * HEAD), jnp.bfloat16)] * groups,
        grid_spec=pltpu.PrefetchScalarGridSpec(
            num_scalar_prefetch=1,
            grid=(heads,),
            in_specs=[own] * 6 + [message] * (groups - 1),
            out_specs=[result] * groups,
        ),
        compiler_params=pltpu.CompilerParams(vmem_limit_bytes=48 * 2**20),
        cost_estimate=pl.CostEstimate(
            flops=heads * 12 * tokens * tokens * HEAD,
            bytes_accessed=heads * 16 * tokens * HEAD,
            transcendentals=heads * tokens * tokens,
        ),
        name="attend",
    )((start // HEAD).astype(jnp.int32)[None], *arrays, *messages)


def on_device(*arrays):
    groups = lax.axis_size("seq")
    me = lax.axis_index("seq")
    span = arrays[0].shape[1] // groups
    sizes = chunk_sizes(span // HEAD)
    rounds = rounds_of(groups)
    to = [jnp.asarray(r, jnp.int32)[me] for r in rounds]
    outs = []
    base = 0
    sent = []
    for heads in sizes:
        width = heads * HEAD
        packed = pack(arrays, [t * span + base for t in to], width)
        received = [
            lax.ppermute(message, "seq", list(enumerate(r))) for message, r in zip(packed, rounds)
        ]
        sent.append((received, base, heads))
        base += width
    for received, base, heads in sent:
        own, *results = attend(arrays, received, me * span + base, heads)
        back = [
            lax.ppermute(message, "seq", [(b, a) for a, b in enumerate(r)])
            for message, r in zip(results, rounds)
        ]
        outs = place(
            outs, [own] + back, [me * span + base] + [t * span + base for t in to], arrays[0].shape
        )
    return tuple(outs)


def solution(mesh):
    spec = P(("dp", "seq"), None)
    return jax.shard_map(
        on_device, mesh=mesh, in_specs=(spec,) * 6, out_specs=(spec, spec), check_vma=False
    )
```

```python
import functools
import math

import jax
import jax.numpy as jnp
from jax import lax
from jax.experimental import pallas as pl
from jax.experimental.pallas import tpu as pltpu
from jax.sharding import PartitionSpec as P

HEAD = 128
ANYWHERE = pl.BlockSpec(memory_space=pl.ANY)
WHOLE = pl.BlockSpec(memory_space=pltpu.VMEM)


def chunk_sizes(count):
    last = max(1, count // 4)
    return [count - last, last] if count > 1 else [count]


def rounds_of(count):
    if count & (count - 1) == 0:
        return [
            (lambda me, step=step: me ^ step, [i ^ step for i in range(count)])
            for step in range(count - 1, 0, -1)
        ]
    return [
        (lambda me, step=step: lax.rem(me + step, count), [(i + step) % count for i in range(count)])
        for step in range(1, count)
    ]


def own_group(me):
    return me


def columns(group, span, base, width):
    start = group(lax.axis_index("seq")) * span + base
    return pl.ds(pl.multiple_of(start, HEAD), width)


def run(copies):
    for copy in copies:
        copy.start()
    for copy in copies:
        copy.wait()


def pack_kernel(groups, span, base, width, *refs):
    arrays, messages, sems = refs[:6], refs[-1 - len(groups):-1], refs[-1]
    run(
        [
            pltpu.make_async_copy(
                arrays[i].at[:, columns(group, span, base, width)],
                messages[m].at[i],
                sems.at[m, i],
            )
            for m, group in enumerate(groups)
            for i in range(6)
        ]
    )


def pack(arrays, groups, span, base, width, after=()):
    count = len(groups)
    rows = arrays[0].shape[0]
    message = jax.ShapeDtypeStruct((6, rows, width), arrays[0].dtype)
    return pl.pallas_call(
        functools.partial(pack_kernel, groups, span, base, width),
        out_shape=[message] * count,
        in_specs=[ANYWHERE] * (6 + len(after)),
        out_specs=[WHOLE] * count,
        scratch_shapes=[pltpu.SemaphoreType.DMA((count, 6))],
        cost_estimate=pl.CostEstimate(
            flops=0, bytes_accessed=count * 24 * rows * width, transcendentals=0
        ),
        name="pack",
    )(*arrays, *after)


def place_kernel(groups, span, base, width, *refs):
    count = len(groups)
    messages, outs, sems = refs[:count], refs[-3:-1], refs[-1]
    run(
        [
            pltpu.make_async_copy(
                messages[m].at[i],
                outs[i].at[:, columns(group, span, base, width)],
                sems.at[m, i],
            )
            for m, group in enumerate(groups)
            for i in range(2)
        ]
    )


def place(outs, messages, groups, span, base, shape):
    count = len(messages)
    _, rows, width = messages[0].shape
    out = jax.ShapeDtypeStruct(shape, messages[0].dtype)
    return pl.pallas_call(
        functools.partial(place_kernel, groups, span, base, width),
        out_shape=[out, out],
        in_specs=[WHOLE] * count + [ANYWHERE] * len(outs),
        out_specs=[ANYWHERE, ANYWHERE],
        scratch_shapes=[pltpu.SemaphoreType.DMA((count, 2))],
        input_output_aliases={count + i: i for i in range(len(outs))},
        cost_estimate=pl.CostEstimate(
            flops=0, bytes_accessed=count * rows * width * 8, transcendentals=0
        ),
        name="place",
    )(*messages, *outs)


def attend_kernel(groups, *refs):
    messages, results = refs[:groups], refs[groups:]

    def joined(which):
        return jnp.concatenate([message[which] for message in messages], axis=0)

    keys = joined(1)
    values = joined(2)
    both_keys = jnp.concatenate([keys, joined(4)], axis=1)
    both_values = jnp.concatenate([values, joined(5)], axis=1)
    width = keys.shape[1]
    scale = width ** -0.5
    across = (((1,), (1,)), ((), ()))
    for message, result in zip(messages, results):
        queries = message[0]
        paired = jnp.concatenate([message[3], queries], axis=1)
        scores = lax.dot_general(queries, keys, across, preferred_element_type=jnp.float32)
        tangent = lax.dot_general(paired, both_keys, across, preferred_element_type=jnp.float32)
        row_max = jnp.max(scores, axis=1, keepdims=True)
        raised = jnp.exp2((scores - row_max) * (scale * math.log2(math.e)))
        exact = raised * (1.0 / jnp.sum(raised, axis=1, keepdims=True))
        weights = exact.astype(jnp.bfloat16)
        mean = jnp.sum(exact * tangent, axis=1, keepdims=True)
        weight_tangent = (exact * ((tangent - mean) * scale)).astype(jnp.bfloat16)
        sums = jnp.dot(weights, both_values, preferred_element_type=jnp.float32)
        moved = jnp.dot(weight_tangent, values, preferred_element_type=jnp.float32)
        result[0] = sums[:, :width].astype(jnp.bfloat16)
        result[1] = (sums[:, width:] + moved).astype(jnp.bfloat16)


def attend(messages):
    groups = len(messages)
    _, rows, width = messages[0].shape
    heads = width // HEAD
    tokens = rows * groups
    return pl.pallas_call(
        functools.partial(attend_kernel, groups),
        out_shape=[jax.ShapeDtypeStruct((2, rows, width), jnp.bfloat16)] * groups,
        grid=(heads,),
        in_specs=[pl.BlockSpec((6, rows, HEAD), lambda h: (0, 0, h))] * groups,
        out_specs=[pl.BlockSpec((2, rows, HEAD), lambda h: (0, 0, h))] * groups,
        compiler_params=pltpu.CompilerParams(vmem_limit_bytes=48 * 2**20),
        cost_estimate=pl.CostEstimate(
            flops=heads * 12 * tokens * tokens * HEAD,
            bytes_accessed=heads * 16 * tokens * HEAD,
            transcendentals=heads * tokens * tokens,
        ),
        name="attend",
    )(*messages)


def on_device(*arrays):
    count = lax.axis_size("seq")
    shape = arrays[0].shape
    span = shape[1] // count
    rounds = rounds_of(count)
    groups = [group for group, _ in rounds]

    def there(message, r):
        return lax.ppermute(message, "seq", list(enumerate(rounds[r][1])))

    def back(message, r):
        return lax.ppermute(message, "seq", [(b, a) for a, b in enumerate(rounds[r][1])])

    chunks = []
    base = 0
    for heads in chunk_sizes(span // HEAD):
        chunks.append((base, heads * HEAD))
        base += heads * HEAD
    received = []
    for base, width in chunks:
        first = pack(arrays, groups[:1], span, base, width)
        rest = pack(arrays, groups[1:], span, base, width)
        own = pack(arrays, [own_group], span, base, width)
        received.append([*own, *(there(m, r) for r, m in enumerate([*first, *rest]))])
    outs = ()
    for (base, width), messages in zip(chunks, received):
        own, *results = attend(messages)
        returned = [back(m, r) for r, m in enumerate(results)]
        outs = place(outs, [own], [own_group], span, base, shape)
        outs = place(outs, returned, groups, span, base, shape)
    return tuple(outs)


def solution(mesh):
    spec = P(("dp", "seq"), None)
    return jax.shard_map(
        on_device, mesh=mesh, in_specs=(spec,) * 6, out_specs=(spec, spec), check_vma=False
    )
```

```python
import functools
import math

import jax
import jax.numpy as jnp
from jax import lax
from jax.experimental import pallas as pl
from jax.experimental.pallas import tpu as pltpu
from jax.sharding import PartitionSpec as P

HEAD = 128
ANYWHERE = pl.BlockSpec(memory_space=pl.ANY)
FAR = pl.BlockSpec(memory_space=pltpu.HBM)
WHOLE = pl.BlockSpec(memory_space=pltpu.VMEM)


def limit(*sizes):
    return pltpu.CompilerParams(vmem_limit_bytes=sum(sizes) + 2**20)


def chunk_sizes(count):
    last = max(1, count // 4)
    return [count - last, last] if count > 1 else [count]


def rounds_of(count):
    if count & (count - 1) == 0:
        return [
            (lambda me, step=step: me ^ step, [i ^ step for i in range(count)])
            for step in range(1, count)
        ]
    return [
        (lambda me, step=step: lax.rem(me + step, count), [(i + step) % count for i in range(count)])
        for step in range(1, count)
    ]


def own_group(me):
    return me


def columns(group, span, base, width):
    start = group(lax.axis_index("seq")) * span + base
    return pl.ds(pl.multiple_of(start, HEAD), width)


def run(copies):
    for copy in copies:
        copy.start()
    for copy in copies:
        copy.wait()


def pack_kernel(groups, count, span, base, width, *refs):
    arrays, messages, sems = refs[:count], refs[-1 - len(groups):-1], refs[-1]
    run(
        [
            pltpu.make_async_copy(
                arrays[i].at[:, columns(group, span, base, width)],
                messages[m].at[i],
                sems.at[m, i],
            )
            for m, group in enumerate(groups)
            for i in range(count)
        ]
    )


def pack(arrays, groups, span, base, width, after=()):
    count = len(arrays)
    rows = arrays[0].shape[0]
    message = pltpu.VMEM((count, rows, width), arrays[0].dtype)
    size = len(groups) * count * rows * width * 2
    return pl.pallas_call(
        functools.partial(pack_kernel, groups, count, span, base, width),
        out_shape=[message] * len(groups),
        in_specs=[FAR] * count + [ANYWHERE] * len(after),
        out_specs=[WHOLE] * len(groups),
        scratch_shapes=[pltpu.SemaphoreType.DMA((len(groups), count))],
        compiler_params=limit(size),
        cost_estimate=pl.CostEstimate(flops=0, bytes_accessed=2 * size, transcendentals=0),
        name="pack",
    )(*(pltpu.with_memory_space_constraint(array, pltpu.HBM) for array in arrays), *after)


def place_kernel(groups, span, base, width, *refs):
    count = len(groups)
    messages, outs, sems = refs[:count], refs[-3:-1], refs[-1]
    run(
        [
            pltpu.make_async_copy(
                messages[m].at[i],
                outs[i].at[:, columns(group, span, base, width)],
                sems.at[m, i],
            )
            for m, group in enumerate(groups)
            for i in range(2)
        ]
    )


def place(outs, messages, groups, span, base, shape):
    count = len(messages)
    _, rows, width = messages[0].shape
    out = jax.ShapeDtypeStruct(shape, messages[0].dtype)
    return pl.pallas_call(
        functools.partial(place_kernel, groups, span, base, width),
        out_shape=[out, out],
        in_specs=[WHOLE] * count + [FAR] * len(outs),
        out_specs=[FAR, FAR],
        scratch_shapes=[pltpu.SemaphoreType.DMA((count, 2))],
        input_output_aliases={count + i: i for i in range(len(outs))},
        compiler_params=limit(count * rows * width * 4),
        cost_estimate=pl.CostEstimate(
            flops=0, bytes_accessed=count * rows * width * 8, transcendentals=0
        ),
        name="place",
    )(*messages, *outs)


def attend_kernel(layout, *refs):
    messages = []
    for counts in layout:
        parts, refs = refs[:len(counts)], refs[len(counts):]
        messages.append([part.at[i] for part, count in zip(parts, counts) for i in range(count)])
    results = refs

    def joined(which):
        return jnp.concatenate([message[which][...] for message in messages], axis=0)

    keys = joined(1)
    values = joined(2)
    both_keys = jnp.concatenate([keys, joined(4)], axis=1)
    both_values = jnp.concatenate([values, joined(5)], axis=1)
    width = keys.shape[1]
    scale = width ** -0.5
    across = (((1,), (1,)), ((), ()))
    for message, result in zip(messages, results):
        queries = message[0][...]
        paired = jnp.concatenate([message[3][...], queries], axis=1)
        scores = lax.dot_general(queries, keys, across, preferred_element_type=jnp.float32)
        tangent = lax.dot_general(paired, both_keys, across, preferred_element_type=jnp.float32)
        row_max = jnp.max(scores, axis=1, keepdims=True)
        raised = jnp.exp2((scores - row_max) * (scale * math.log2(math.e)))
        exact = raised * (1.0 / jnp.sum(raised, axis=1, keepdims=True))
        weights = exact.astype(jnp.bfloat16)
        mean = jnp.sum(exact * tangent, axis=1, keepdims=True)
        weight_tangent = (exact * ((tangent - mean) * scale)).astype(jnp.bfloat16)
        sums = jnp.dot(weights, both_values, preferred_element_type=jnp.float32)
        moved = jnp.dot(weight_tangent, values, preferred_element_type=jnp.float32)
        result[0] = sums[:, :width].astype(jnp.bfloat16)
        result[1] = (sums[:, width:] + moved).astype(jnp.bfloat16)


def attend(messages):
    groups = len(messages)
    parts = [part for message in messages for part in message]
    layout = [[part.shape[0] for part in message] for message in messages]
    _, rows, width = parts[0].shape
    heads = width // HEAD
    tokens = rows * groups
    return pl.pallas_call(
        functools.partial(attend_kernel, layout),
        out_shape=[jax.ShapeDtypeStruct((2, rows, width), jnp.bfloat16)] * groups,
        grid=(heads,),
        in_specs=[
            pl.BlockSpec((part.shape[0], rows, HEAD), lambda h: (0, 0, h)) for part in parts
        ],
        out_specs=[pl.BlockSpec((2, rows, HEAD), lambda h: (0, 0, h))] * groups,
        compiler_params=limit(32 * tokens * HEAD * 2, 32 * rows * tokens * 4),
        cost_estimate=pl.CostEstimate(
            flops=heads * 12 * tokens * tokens * HEAD,
            bytes_accessed=heads * 16 * tokens * HEAD,
            transcendentals=heads * tokens * tokens,
        ),
        name="attend",
    )(*parts)


def on_device(*arrays):
    count = lax.axis_size("seq")
    shape = arrays[0].shape
    span = shape[1] // count
    rounds = rounds_of(count)
    groups = [group for group, _ in rounds]

    def there(message, r):
        return lax.ppermute(message, "seq", list(enumerate(rounds[r][1])))

    def back(message, r):
        return lax.ppermute(message, "seq", [(b, a) for a, b in enumerate(rounds[r][1])])

    chunks = []
    base = 0
    for heads in chunk_sizes(span // HEAD):
        chunks.append((base, heads * HEAD))
        base += heads * HEAD
    received = []
    for base, width in chunks:
        sent = [pack(arrays, [group], span, base, width) for group in groups]
        own = pack(arrays, [own_group], span, base, width, after=sent[-1])
        received.append([own, *([there(part, r) for part in m] for r, m in enumerate(sent))])
    outs = ()
    for (base, width), messages in zip(chunks, received):
        own, *results = attend(messages)
        returned = [back(m, r) for r, m in enumerate(results)]
        outs = place(outs, [own], [own_group], span, base, shape)
        outs = place(outs, returned, groups, span, base, shape)
    return tuple(outs)


def solution(mesh):
    spec = P(("dp", "seq"), None)
    return jax.shard_map(
        on_device, mesh=mesh, in_specs=(spec,) * 6, out_specs=(spec, spec), check_vma=False
    )
```

```python
import functools
import math

import jax
import jax.numpy as jnp
from jax import lax
from jax.experimental import pallas as pl
from jax.experimental.pallas import tpu as pltpu
from jax.sharding import PartitionSpec as P

HEAD = 128
ANYWHERE = pl.BlockSpec(memory_space=pl.ANY)
FAR = pl.BlockSpec(memory_space=pltpu.HBM)
WHOLE = pl.BlockSpec(memory_space=pltpu.VMEM)


def limit(*sizes):
    return pltpu.CompilerParams(vmem_limit_bytes=sum(sizes) + 2**20)


def chunk_sizes(count):
    last = max(1, 3 * count // 8)
    return [count - last, last] if count > 1 else [count]


def rounds_of(count):
    if count & (count - 1) == 0:
        return [
            (lambda me, step=step: me ^ step, [i ^ step for i in range(count)])
            for step in range(1, count)
        ]
    return [
        (lambda me, step=step: lax.rem(me + step, count), [(i + step) % count for i in range(count)])
        for step in range(1, count)
    ]


def own_group(me):
    return me


def columns(group, span, base, width):
    start = group(lax.axis_index("seq")) * span + base
    return pl.ds(pl.multiple_of(start, HEAD), width)


def run(copies):
    for copy in copies:
        copy.start()
    for copy in copies:
        copy.wait()


def pack_kernel(groups, count, span, base, width, *refs):
    arrays, messages, sems = refs[:count], refs[-1 - len(groups):-1], refs[-1]
    run(
        [
            pltpu.make_async_copy(
                arrays[i].at[:, columns(group, span, base, width)],
                messages[m].at[i],
                sems.at[m, i],
            )
            for m, group in enumerate(groups)
            for i in range(count)
        ]
    )


def pack(arrays, groups, span, base, width, after=()):
    count = len(arrays)
    rows = arrays[0].shape[0]
    message = pltpu.VMEM((count, rows, width), arrays[0].dtype)
    size = len(groups) * count * rows * width * 2
    return pl.pallas_call(
        functools.partial(pack_kernel, groups, count, span, base, width),
        out_shape=[message] * len(groups),
        in_specs=[FAR] * count + [ANYWHERE] * len(after),
        out_specs=[WHOLE] * len(groups),
        scratch_shapes=[pltpu.SemaphoreType.DMA((len(groups), count))],
        compiler_params=limit(size),
        cost_estimate=pl.CostEstimate(flops=0, bytes_accessed=2 * size, transcendentals=0),
        name="pack",
    )(*(pltpu.with_memory_space_constraint(array, pltpu.HBM) for array in arrays), *after)


def place_kernel(groups, span, base, width, *refs):
    count = len(groups)
    messages, outs, sems = refs[:count], refs[-3:-1], refs[-1]
    run(
        [
            pltpu.make_async_copy(
                messages[m].at[i],
                outs[i].at[:, columns(group, span, base, width)],
                sems.at[m, i],
            )
            for m, group in enumerate(groups)
            for i in range(2)
        ]
    )


def place(outs, messages, groups, span, base, shape):
    count = len(messages)
    _, rows, width = messages[0].shape
    out = jax.ShapeDtypeStruct(shape, messages[0].dtype)
    return pl.pallas_call(
        functools.partial(place_kernel, groups, span, base, width),
        out_shape=[out, out],
        in_specs=[WHOLE] * count + [FAR] * len(outs),
        out_specs=[FAR, FAR],
        scratch_shapes=[pltpu.SemaphoreType.DMA((count, 2))],
        input_output_aliases={count + i: i for i in range(len(outs))},
        compiler_params=limit(count * rows * width * 4),
        cost_estimate=pl.CostEstimate(
            flops=0, bytes_accessed=count * rows * width * 8, transcendentals=0
        ),
        name="place",
    )(*messages, *outs)


def attend_kernel(layout, *refs):
    messages = []
    for counts in layout:
        parts, refs = refs[:len(counts)], refs[len(counts):]
        messages.append([part.at[i] for part, count in zip(parts, counts) for i in range(count)])
    results = refs

    def joined(which):
        return jnp.concatenate([message[which][...] for message in messages], axis=0)

    keys = joined(1)
    values = joined(2)
    both_keys = jnp.concatenate([keys, joined(4)], axis=1)
    both_values = jnp.concatenate([values, joined(5)], axis=1)
    width = keys.shape[1]
    scale = width ** -0.5
    across = (((1,), (1,)), ((), ()))
    for message, result in zip(messages, results):
        queries = message[0][...]
        paired = jnp.concatenate([message[3][...], queries], axis=1)
        scores = lax.dot_general(queries, keys, across, preferred_element_type=jnp.float32)
        tangent = lax.dot_general(paired, both_keys, across, preferred_element_type=jnp.float32)
        row_max = jnp.max(scores, axis=1, keepdims=True)
        raised = jnp.exp2((scores - row_max) * (scale * math.log2(math.e)))
        exact = raised * (1.0 / jnp.sum(raised, axis=1, keepdims=True))
        weights = exact.astype(jnp.bfloat16)
        mean = jnp.sum(exact * tangent, axis=1, keepdims=True)
        weight_tangent = (exact * ((tangent - mean) * scale)).astype(jnp.bfloat16)
        sums = jnp.dot(weights, both_values, preferred_element_type=jnp.float32)
        moved = jnp.dot(weight_tangent, values, preferred_element_type=jnp.float32)
        result[0] = sums[:, :width].astype(jnp.bfloat16)
        result[1] = (sums[:, width:] + moved).astype(jnp.bfloat16)


def attend(messages):
    groups = len(messages)
    parts = [part for message in messages for part in message]
    layout = [[part.shape[0] for part in message] for message in messages]
    _, rows, width = parts[0].shape
    heads = width // HEAD
    tokens = rows * groups
    return pl.pallas_call(
        functools.partial(attend_kernel, layout),
        out_shape=[jax.ShapeDtypeStruct((2, rows, width), jnp.bfloat16)] * groups,
        grid=(heads,),
        in_specs=[
            pl.BlockSpec((part.shape[0], rows, HEAD), lambda h: (0, 0, h)) for part in parts
        ],
        out_specs=[pl.BlockSpec((2, rows, HEAD), lambda h: (0, 0, h))] * groups,
        compiler_params=limit(32 * tokens * HEAD * 2, 32 * rows * tokens * 4),
        cost_estimate=pl.CostEstimate(
            flops=heads * 12 * tokens * tokens * HEAD,
            bytes_accessed=heads * 16 * tokens * HEAD,
            transcendentals=heads * tokens * tokens,
        ),
        name="attend",
    )(*parts)


def on_device(*arrays):
    count = lax.axis_size("seq")
    shape = arrays[0].shape
    span = shape[1] // count
    rounds = rounds_of(count)
    groups = [group for group, _ in rounds]

    def there(message, r):
        return lax.ppermute(message, "seq", list(enumerate(rounds[r][1])))

    def back(message, r):
        return lax.ppermute(message, "seq", [(b, a) for a, b in enumerate(rounds[r][1])])

    chunks = []
    base = 0
    for heads in chunk_sizes(span // HEAD):
        chunks.append((base, heads * HEAD))
        base += heads * HEAD
    received = []
    for base, width in chunks:
        sent = [pack(arrays, [group], span, base, width) for group in groups]
        own = pack(arrays, [own_group], span, base, width, after=sent[-1])
        received.append([own, *([there(part, r) for part in m] for r, m in enumerate(sent))])
    outs = ()
    for (base, width), messages in zip(chunks, received):
        own, *results = attend(messages)
        returned = [back(m, r) for r, m in enumerate(results)]
        outs = place(outs, [own], [own_group], span, base, shape)
        for group, message in zip(groups, returned):
            outs = place(outs, [message], [group], span, base, shape)
    return tuple(outs)


def solution(mesh):
    spec = P(("dp", "seq"), None)
    return jax.shard_map(
        on_device, mesh=mesh, in_specs=(spec,) * 6, out_specs=(spec, spec), check_vma=False
    )
```

```python
import functools
import math

import jax
import jax.numpy as jnp
from jax import lax
from jax.experimental import pallas as pl
from jax.experimental.pallas import tpu as pltpu
from jax.sharding import PartitionSpec as P

HEAD = 128
ANYWHERE = pl.BlockSpec(memory_space=pl.ANY)
FAR = pl.BlockSpec(memory_space=pltpu.HBM)
WHOLE = pl.BlockSpec(memory_space=pltpu.VMEM)


def limit(*sizes):
    return pltpu.CompilerParams(vmem_limit_bytes=sum(sizes) + 2**20)


def chunk_sizes(count):
    last = max(1, 3 * count // 8)
    return [count - last, last] if count > 1 else [count]


def rounds_of(count):
    if count & (count - 1) == 0 and count > 2:
        half = count // 2

        def partner(step, me):
            return me ^ step if step < half else me ^ step ^ lax.div(me, half)

        def static(step, i):
            return i ^ step if step < half else i ^ step ^ (i // half)

        return [
            (functools.partial(partner, step), [static(step, i) for i in range(count)])
            for step in range(1, count)
        ]
    return [
        (lambda me, step=step: lax.rem(me + step, count), [(i + step) % count for i in range(count)])
        for step in range(1, count)
    ]


def own_group(me):
    return me


def columns(group, span, base, width):
    start = group(lax.axis_index("seq")) * span + base
    return pl.ds(pl.multiple_of(start, HEAD), width)


def run(copies):
    for copy in copies:
        copy.start()
    for copy in copies:
        copy.wait()


def pack_kernel(groups, count, span, base, width, *refs):
    arrays, messages, sems = refs[:count], refs[-1 - len(groups):-1], refs[-1]
    run(
        [
            pltpu.make_async_copy(
                arrays[i].at[:, columns(group, span, base, width)],
                messages[m].at[i],
                sems.at[m, i],
            )
            for m, group in enumerate(groups)
            for i in range(count)
        ]
    )


def pack(arrays, groups, span, base, width, after=()):
    count = len(arrays)
    rows = arrays[0].shape[0]
    message = pltpu.VMEM((count, rows, width), arrays[0].dtype)
    size = len(groups) * count * rows * width * 2
    return pl.pallas_call(
        functools.partial(pack_kernel, groups, count, span, base, width),
        out_shape=[message] * len(groups),
        in_specs=[FAR] * count + [ANYWHERE] * len(after),
        out_specs=[WHOLE] * len(groups),
        scratch_shapes=[pltpu.SemaphoreType.DMA((len(groups), count))],
        compiler_params=limit(size),
        cost_estimate=pl.CostEstimate(flops=0, bytes_accessed=2 * size, transcendentals=0),
        name="pack",
    )(*(pltpu.with_memory_space_constraint(array, pltpu.HBM) for array in arrays), *after)


def place_kernel(groups, span, base, width, *refs):
    count = len(groups)
    messages, outs, sems = refs[:count], refs[-3:-1], refs[-1]
    run(
        [
            pltpu.make_async_copy(
                messages[m].at[i],
                outs[i].at[:, columns(group, span, base, width)],
                sems.at[m, i],
            )
            for m, group in enumerate(groups)
            for i in range(2)
        ]
    )


def place(outs, messages, groups, span, base, shape):
    count = len(messages)
    _, rows, width = messages[0].shape
    out = jax.ShapeDtypeStruct(shape, messages[0].dtype)
    return pl.pallas_call(
        functools.partial(place_kernel, groups, span, base, width),
        out_shape=[out, out],
        in_specs=[WHOLE] * count + [FAR] * len(outs),
        out_specs=[FAR, FAR],
        scratch_shapes=[pltpu.SemaphoreType.DMA((count, 2))],
        input_output_aliases={count + i: i for i in range(len(outs))},
        compiler_params=limit(count * rows * width * 4),
        cost_estimate=pl.CostEstimate(
            flops=0, bytes_accessed=count * rows * width * 8, transcendentals=0
        ),
        name="place",
    )(*messages, *outs)


def attend_kernel(layout, *refs):
    messages = []
    for counts in layout:
        parts, refs = refs[:len(counts)], refs[len(counts):]
        messages.append([part.at[i] for part, count in zip(parts, counts) for i in range(count)])
    results = refs

    def joined(which):
        return jnp.concatenate([message[which][...] for message in messages], axis=0)

    keys = joined(1)
    values = joined(2)
    both_keys = jnp.concatenate([keys, joined(4)], axis=1)
    both_values = jnp.concatenate([values, joined(5)], axis=1)
    width = keys.shape[1]
    scale = width ** -0.5
    across = (((1,), (1,)), ((), ()))
    for message, result in zip(messages, results):
        queries = message[0][...]
        paired = jnp.concatenate([message[3][...], queries], axis=1)
        scores = lax.dot_general(queries, keys, across, preferred_element_type=jnp.float32)
        tangent = lax.dot_general(paired, both_keys, across, preferred_element_type=jnp.float32)
        row_max = jnp.max(scores, axis=1, keepdims=True)
        raised = jnp.exp2((scores - row_max) * (scale * math.log2(math.e)))
        exact = raised * (1.0 / jnp.sum(raised, axis=1, keepdims=True))
        weights = exact.astype(jnp.bfloat16)
        mean = jnp.sum(exact * tangent, axis=1, keepdims=True)
        weight_tangent = (exact * ((tangent - mean) * scale)).astype(jnp.bfloat16)
        sums = jnp.dot(weights, both_values, preferred_element_type=jnp.float32)
        moved = jnp.dot(weight_tangent, values, preferred_element_type=jnp.float32)
        result[0] = sums[:, :width].astype(jnp.bfloat16)
        result[1] = (sums[:, width:] + moved).astype(jnp.bfloat16)


def attend(messages):
    groups = len(messages)
    parts = [part for message in messages for part in message]
    layout = [[part.shape[0] for part in message] for message in messages]
    _, rows, width = parts[0].shape
    heads = width // HEAD
    tokens = rows * groups
    return pl.pallas_call(
        functools.partial(attend_kernel, layout),
        out_shape=[jax.ShapeDtypeStruct((2, rows, width), jnp.bfloat16)] * groups,
        grid=(heads,),
        in_specs=[
            pl.BlockSpec((part.shape[0], rows, HEAD), lambda h: (0, 0, h)) for part in parts
        ],
        out_specs=[pl.BlockSpec((2, rows, HEAD), lambda h: (0, 0, h))] * groups,
        compiler_params=limit(32 * tokens * HEAD * 2, 32 * rows * tokens * 4),
        cost_estimate=pl.CostEstimate(
            flops=heads * 12 * tokens * tokens * HEAD,
            bytes_accessed=heads * 16 * tokens * HEAD,
            transcendentals=heads * tokens * tokens,
        ),
        name="attend",
    )(*parts)


def on_device(*arrays):
    count = lax.axis_size("seq")
    shape = arrays[0].shape
    span = shape[1] // count
    rounds = rounds_of(count)
    groups = [group for group, _ in rounds]

    def there(message, r):
        return lax.ppermute(message, "seq", list(enumerate(rounds[r][1])))

    def back(message, r):
        return lax.ppermute(message, "seq", [(b, a) for a, b in enumerate(rounds[r][1])])

    chunks = []
    base = 0
    for heads in chunk_sizes(span // HEAD):
        chunks.append((base, heads * HEAD))
        base += heads * HEAD
    received = []
    for base, width in chunks:
        sent = [pack(arrays, [group], span, base, width) for group in groups]
        own = pack(arrays, [own_group], span, base, width, after=sent[-1])
        received.append([own, *([there(part, r) for part in m] for r, m in enumerate(sent))])
    outs = ()
    for (base, width), messages in zip(chunks, received):
        own, *results = attend(messages)
        returned = [back(m, r) for r, m in enumerate(results)]
        outs = place(outs, [own], [own_group], span, base, shape)
        for group, message in zip(groups, returned):
            outs = place(outs, [message], [group], span, base, shape)
    return tuple(outs)


def solution(mesh):
    spec = P(("dp", "seq"), None)
    return jax.shard_map(
        on_device, mesh=mesh, in_specs=(spec,) * 6, out_specs=(spec, spec), check_vma=False
    )
```

```python
import functools
import math

import jax
import jax.numpy as jnp
from jax import lax
from jax.experimental import pallas as pl
from jax.experimental.pallas import tpu as pltpu
from jax.sharding import PartitionSpec as P

HEAD = 128
ANYWHERE = pl.BlockSpec(memory_space=pl.ANY)
FAR = pl.BlockSpec(memory_space=pltpu.HBM)
WHOLE = pl.BlockSpec(memory_space=pltpu.VMEM)


def limit(*sizes):
    return pltpu.CompilerParams(vmem_limit_bytes=sum(sizes) + 2**20)


def chunk_sizes(count):
    last = max(1, 3 * count // 8)
    return [count - last, last] if count > 1 else [count]


def rounds_of(count):
    if count & (count - 1) == 0 and count > 2:
        half = count // 2

        def partner(step, me):
            return me ^ step if step < half else me ^ step ^ lax.div(me, half)

        def static(step, i):
            return i ^ step if step < half else i ^ step ^ (i // half)

        return [
            (functools.partial(partner, step), [static(step, i) for i in range(count)])
            for step in range(1, count)
        ]
    return [
        (lambda me, step=step: lax.rem(me + step, count), [(i + step) % count for i in range(count)])
        for step in range(1, count)
    ]


def own_group(me):
    return me


def columns(group, span, base, width):
    start = group(lax.axis_index("seq")) * span + base
    return pl.ds(pl.multiple_of(start, HEAD), width)


def run(copies):
    for copy in copies:
        copy.start()
    for copy in copies:
        copy.wait()


def pack_kernel(groups, count, span, base, width, *refs):
    arrays, messages, sem = refs[:count], refs[-1 - len(groups):-1], refs[-1]
    rows = arrays[0].shape[0]
    slabs = math.gcd(rows // 16, 4) if rows % 16 == 0 else 1
    for m, group in enumerate(groups):
        for i in range(count):
            for j in range(slabs):
                slab = pl.ds(j * (rows // slabs), rows // slabs)
                pltpu.make_async_copy(
                    arrays[i].at[slab, columns(group, span, base, width)],
                    messages[m].at[i, slab],
                    sem.at[m],
                ).start()
    for m in range(len(groups)):
        pltpu.make_async_copy(messages[m], messages[m], sem.at[m]).wait()


def pack(arrays, groups, span, base, width, after=()):
    count = len(arrays)
    rows = arrays[0].shape[0]
    message = pltpu.VMEM((count, rows, width), arrays[0].dtype)
    size = len(groups) * count * rows * width * 2
    return pl.pallas_call(
        functools.partial(pack_kernel, groups, count, span, base, width),
        out_shape=[message] * len(groups),
        in_specs=[FAR] * count + [ANYWHERE] * len(after),
        out_specs=[WHOLE] * len(groups),
        scratch_shapes=[pltpu.SemaphoreType.DMA((len(groups),))],
        compiler_params=limit(size),
        cost_estimate=pl.CostEstimate(flops=0, bytes_accessed=2 * size, transcendentals=0),
        name="pack",
    )(*(pltpu.with_memory_space_constraint(array, pltpu.HBM) for array in arrays), *after)


def place_kernel(groups, span, base, width, *refs):
    count = len(groups)
    messages, outs, sems = refs[:count], refs[-3:-1], refs[-1]
    run(
        [
            pltpu.make_async_copy(
                messages[m].at[i],
                outs[i].at[:, columns(group, span, base, width)],
                sems.at[m, i],
            )
            for m, group in enumerate(groups)
            for i in range(2)
        ]
    )


def place(outs, messages, groups, span, base, shape):
    count = len(messages)
    _, rows, width = messages[0].shape
    out = jax.ShapeDtypeStruct(shape, messages[0].dtype)
    return pl.pallas_call(
        functools.partial(place_kernel, groups, span, base, width),
        out_shape=[out, out],
        in_specs=[WHOLE] * count + [FAR] * len(outs),
        out_specs=[FAR, FAR],
        scratch_shapes=[pltpu.SemaphoreType.DMA((count, 2))],
        input_output_aliases={count + i: i for i in range(len(outs))},
        compiler_params=limit(count * rows * width * 4),
        cost_estimate=pl.CostEstimate(
            flops=0, bytes_accessed=count * rows * width * 8, transcendentals=0
        ),
        name="place",
    )(*messages, *outs)


def attend_kernel(layout, *refs):
    messages = []
    for counts in layout:
        parts, refs = refs[:len(counts)], refs[len(counts):]
        messages.append([part.at[i] for part, count in zip(parts, counts) for i in range(count)])
    results = refs

    def joined(which):
        return jnp.concatenate([message[which][...] for message in messages], axis=0)

    keys = joined(1)
    values = joined(2)
    both_keys = jnp.concatenate([keys, joined(4)], axis=1)
    both_values = jnp.concatenate([values, joined(5)], axis=1)
    width = keys.shape[1]
    scale = width ** -0.5
    across = (((1,), (1,)), ((), ()))
    for message, result in zip(messages, results):
        queries = message[0][...]
        paired = jnp.concatenate([message[3][...], queries], axis=1)
        scores = lax.dot_general(queries, keys, across, preferred_element_type=jnp.float32)
        tangent = lax.dot_general(paired, both_keys, across, preferred_element_type=jnp.float32)
        row_max = jnp.max(scores, axis=1, keepdims=True)
        raised = jnp.exp2((scores - row_max) * (scale * math.log2(math.e)))
        exact = raised * (1.0 / jnp.sum(raised, axis=1, keepdims=True))
        weights = exact.astype(jnp.bfloat16)
        mean = jnp.sum(exact * tangent, axis=1, keepdims=True)
        weight_tangent = (exact * ((tangent - mean) * scale)).astype(jnp.bfloat16)
        sums = jnp.dot(weights, both_values, preferred_element_type=jnp.float32)
        moved = jnp.dot(weight_tangent, values, preferred_element_type=jnp.float32)
        result[0] = sums[:, :width].astype(jnp.bfloat16)
        result[1] = (sums[:, width:] + moved).astype(jnp.bfloat16)


def attend(messages):
    groups = len(messages)
    parts = [part for message in messages for part in message]
    layout = [[part.shape[0] for part in message] for message in messages]
    _, rows, width = parts[0].shape
    heads = width // HEAD
    tokens = rows * groups
    return pl.pallas_call(
        functools.partial(attend_kernel, layout),
        out_shape=[jax.ShapeDtypeStruct((2, rows, width), jnp.bfloat16)] * groups,
        grid=(heads,),
        in_specs=[
            pl.BlockSpec((part.shape[0], rows, HEAD), lambda h: (0, 0, h)) for part in parts
        ],
        out_specs=[pl.BlockSpec((2, rows, HEAD), lambda h: (0, 0, h))] * groups,
        compiler_params=limit(32 * tokens * HEAD * 2, 32 * rows * tokens * 4),
        cost_estimate=pl.CostEstimate(
            flops=heads * 12 * tokens * tokens * HEAD,
            bytes_accessed=heads * 16 * tokens * HEAD,
            transcendentals=heads * tokens * tokens,
        ),
        name="attend",
    )(*parts)


def on_device(*arrays):
    count = lax.axis_size("seq")
    shape = arrays[0].shape
    span = shape[1] // count
    rounds = rounds_of(count)
    groups = [group for group, _ in rounds]

    def there(message, r):
        return lax.ppermute(message, "seq", list(enumerate(rounds[r][1])))

    def back(message, r):
        return lax.ppermute(message, "seq", [(b, a) for a, b in enumerate(rounds[r][1])])

    chunks = []
    base = 0
    for heads in chunk_sizes(span // HEAD):
        chunks.append((base, heads * HEAD))
        base += heads * HEAD
    received = []
    for base, width in chunks:
        sent = [pack(arrays, [group], span, base, width) for group in groups]
        own = pack(arrays, [own_group], span, base, width, after=sent[-1])
        received.append([own, *([there(part, r) for part in m] for r, m in enumerate(sent))])
    outs = ()
    for (base, width), messages in zip(chunks, received):
        own, *results = attend(messages)
        returned = [back(m, r) for r, m in enumerate(results)]
        outs = place(outs, [own], [own_group], span, base, shape)
        for group, message in zip(groups, returned):
            outs = place(outs, [message], [group], span, base, shape)
    return tuple(outs)


def solution(mesh):
    spec = P(("dp", "seq"), None)
    return jax.shard_map(
        on_device, mesh=mesh, in_specs=(spec,) * 6, out_specs=(spec, spec), check_vma=False
    )
```

```python
import functools
import math

import jax
import jax.numpy as jnp
from jax import lax
from jax.experimental import pallas as pl
from jax.experimental.pallas import tpu as pltpu
from jax.sharding import PartitionSpec as P

HEAD = 128
ANYWHERE = pl.BlockSpec(memory_space=pl.ANY)
FAR = pl.BlockSpec(memory_space=pltpu.HBM)
WHOLE = pl.BlockSpec(memory_space=pltpu.VMEM)


def limit(*sizes):
    return pltpu.CompilerParams(vmem_limit_bytes=sum(sizes) + 2**20)


def chunk_sizes(count):
    last = max(1, 3 * count // 8)
    return [count - last, last] if count > 1 else [count]


def rounds_of(count):
    if count & (count - 1) == 0 and count > 2:
        half = count // 2

        def partner(step, me):
            return me ^ step if step < half else me ^ step ^ lax.div(me, half)

        def static(step, i):
            return i ^ step if step < half else i ^ step ^ (i // half)

        return [
            (functools.partial(partner, step), [static(step, i) for i in range(count)])
            for step in range(1, count)
        ]
    return [
        (lambda me, step=step: lax.rem(me + step, count), [(i + step) % count for i in range(count)])
        for step in range(1, count)
    ]


def own_group(me):
    return me


def columns(group, span, base, width):
    start = group(lax.axis_index("seq")) * span + base
    return pl.ds(pl.multiple_of(start, HEAD), width)


def run(copies):
    for copy in copies:
        copy.start()
    for copy in copies:
        copy.wait()


def pack_kernel(groups, count, span, base, width, *refs):
    arrays, messages, sem = refs[:count], refs[-1 - len(groups):-1], refs[-1]
    rows = arrays[0].shape[0]
    slabs = math.gcd(rows // 16, 4) if rows % 16 == 0 else 1
    for m, group in enumerate(groups):
        for i in range(count):
            for j in range(slabs):
                slab = pl.ds(j * (rows // slabs), rows // slabs)
                pltpu.make_async_copy(
                    arrays[i].at[slab, columns(group, span, base, width)],
                    messages[m].at[i, slab],
                    sem.at[m],
                ).start()
    for m in range(len(groups)):
        pltpu.make_async_copy(messages[m], messages[m], sem.at[m]).wait()


def pack(arrays, groups, span, base, width, after=()):
    count = len(arrays)
    rows = arrays[0].shape[0]
    message = pltpu.VMEM((count, rows, width), arrays[0].dtype)
    size = len(groups) * count * rows * width * 2
    return pl.pallas_call(
        functools.partial(pack_kernel, groups, count, span, base, width),
        out_shape=[message] * len(groups),
        in_specs=[FAR] * count + [ANYWHERE] * len(after),
        out_specs=[WHOLE] * len(groups),
        scratch_shapes=[pltpu.SemaphoreType.DMA((len(groups),))],
        compiler_params=limit(size),
        cost_estimate=pl.CostEstimate(flops=0, bytes_accessed=2 * size, transcendentals=0),
        name="pack",
    )(*(pltpu.with_memory_space_constraint(array, pltpu.HBM) for array in arrays), *after)


def place_kernel(groups, span, base, width, *refs):
    count = len(groups)
    messages, outs, sems = refs[:count], refs[-3:-1], refs[-1]
    run(
        [
            pltpu.make_async_copy(
                messages[m].at[i],
                outs[i].at[:, columns(group, span, base, width)],
                sems.at[m, i],
            )
            for m, group in enumerate(groups)
            for i in range(2)
        ]
    )


def place(outs, messages, groups, span, base, shape):
    count = len(messages)
    _, rows, width = messages[0].shape
    out = jax.ShapeDtypeStruct(shape, messages[0].dtype)
    return pl.pallas_call(
        functools.partial(place_kernel, groups, span, base, width),
        out_shape=[out, out],
        in_specs=[WHOLE] * count + [FAR] * len(outs),
        out_specs=[FAR, FAR],
        scratch_shapes=[pltpu.SemaphoreType.DMA((count, 2))],
        input_output_aliases={count + i: i for i in range(len(outs))},
        compiler_params=limit(count * rows * width * 4),
        cost_estimate=pl.CostEstimate(
            flops=0, bytes_accessed=count * rows * width * 8, transcendentals=0
        ),
        name="place",
    )(*messages, *outs)


def attend_kernel(layout, *refs):
    messages = []
    for counts in layout:
        parts, refs = refs[:len(counts)], refs[len(counts):]
        messages.append([part.at[i] for part, count in zip(parts, counts) for i in range(count)])
    results = refs

    def joined(which):
        return jnp.concatenate([message[which][...] for message in messages], axis=0)

    keys = joined(1)
    values = joined(2)
    both_keys = jnp.concatenate([keys, joined(4)], axis=1)
    both_values = jnp.concatenate([values, joined(5)], axis=1)
    width = keys.shape[1]
    scale = width ** -0.5
    across = (((1,), (1,)), ((), ()))
    for message, result in zip(messages, results):
        queries = message[0][...]
        paired = jnp.concatenate([message[3][...], queries], axis=1)
        scores = lax.dot_general(queries, keys, across, preferred_element_type=jnp.float32)
        tangent = lax.dot_general(paired, both_keys, across, preferred_element_type=jnp.float32)
        row_max = jnp.max(scores, axis=1, keepdims=True)
        raised = jnp.exp2((scores - row_max) * (scale * math.log2(math.e)))
        exact = raised * (1.0 / jnp.sum(raised, axis=1, keepdims=True))
        weights = exact.astype(jnp.bfloat16)
        mean = jnp.sum(exact * tangent, axis=1, keepdims=True)
        weight_tangent = (exact * ((tangent - mean) * scale)).astype(jnp.bfloat16)
        sums = jnp.dot(weights, both_values, preferred_element_type=jnp.float32)
        moved = jnp.dot(weight_tangent, values, preferred_element_type=jnp.float32)
        result[0] = sums[:, :width].astype(jnp.bfloat16)
        result[1] = (sums[:, width:] + moved).astype(jnp.bfloat16)


def attend(messages):
    groups = len(messages)
    parts = [part for message in messages for part in message]
    layout = [[part.shape[0] for part in message] for message in messages]
    _, rows, width = parts[0].shape
    heads = width // HEAD
    tokens = rows * groups
    return pl.pallas_call(
        functools.partial(attend_kernel, layout),
        out_shape=[jax.ShapeDtypeStruct((2, rows, width), jnp.bfloat16)] * groups,
        grid=(heads,),
        in_specs=[
            pl.BlockSpec((part.shape[0], rows, HEAD), lambda h: (0, 0, h)) for part in parts
        ],
        out_specs=[pl.BlockSpec((2, rows, HEAD), lambda h: (0, 0, h))] * groups,
        compiler_params=limit(32 * tokens * HEAD * 2, 32 * rows * tokens * 4),
        cost_estimate=pl.CostEstimate(
            flops=heads * 12 * tokens * tokens * HEAD,
            bytes_accessed=heads * 16 * tokens * HEAD,
            transcendentals=heads * tokens * tokens,
        ),
        name="attend",
    )(*parts)


def on_device(*arrays):
    count = lax.axis_size("seq")
    shape = arrays[0].shape
    span = shape[1] // count
    rounds = rounds_of(count)
    groups = [group for group, _ in rounds]

    def there(message, r):
        return lax.ppermute(message, "seq", list(enumerate(rounds[r][1])))

    def back(message, r):
        return lax.ppermute(message, "seq", [(b, a) for a, b in enumerate(rounds[r][1])])

    chunks = []
    base = 0
    for heads in chunk_sizes(span // HEAD):
        chunks.append((base, heads * HEAD))
        base += heads * HEAD
    received = []
    for base, width in chunks:
        parts = [arrays[:4], arrays[4:]] if base == 0 else [arrays]
        sent = [[*(pack(part, [group], span, base, width)[0] for part in parts)] for group in groups]
        own = pack(arrays, [own_group], span, base, width, after=sent[-1])
        received.append([own, *([there(part, r) for part in m] for r, m in enumerate(sent))])
    outs = ()
    for (base, width), messages in zip(chunks, received):
        own, *results = attend(messages)
        returned = [back(m, r) for r, m in enumerate(results)]
        outs = place(outs, [own], [own_group], span, base, shape)
        for group, message in zip(groups, returned):
            outs = place(outs, [message], [group], span, base, shape)
    return tuple(outs)


def solution(mesh):
    spec = P(("dp", "seq"), None)
    return jax.shard_map(
        on_device, mesh=mesh, in_specs=(spec,) * 6, out_specs=(spec, spec), check_vma=False
    )
```

```python
import functools
import math

import jax
import jax.numpy as jnp
from jax import lax
from jax.experimental import pallas as pl
from jax.experimental.pallas import tpu as pltpu
from jax.sharding import PartitionSpec as P

HEAD = 128
ANYWHERE = pl.BlockSpec(memory_space=pl.ANY)
FAR = pl.BlockSpec(memory_space=pltpu.HBM)
WHOLE = pl.BlockSpec(memory_space=pltpu.VMEM)


def limit(*sizes):
    return pltpu.CompilerParams(vmem_limit_bytes=sum(sizes) + 2**20)


def chunk_sizes(count):
    last = max(1, 3 * count // 8)
    return [count - last, last] if count > 1 else [count]


def rounds_of(count):
    if count & (count - 1) == 0 and count > 2:
        half = count // 2

        def partner(step, me):
            return me ^ step if step < half else me ^ step ^ lax.div(me, half)

        def static(step, i):
            return i ^ step if step < half else i ^ step ^ (i // half)

        return [
            (functools.partial(partner, step), [static(step, i) for i in range(count)])
            for step in range(1, count)
        ]
    return [
        (lambda me, step=step: lax.rem(me + step, count), [(i + step) % count for i in range(count)])
        for step in range(1, count)
    ]


def own_group(me):
    return me


def columns(group, span, base, width):
    start = group(lax.axis_index("seq")) * span + base
    return pl.ds(pl.multiple_of(start, HEAD), width)


def run(copies):
    for copy in copies:
        copy.start()
    for copy in copies:
        copy.wait()


def pack_kernel(groups, count, span, base, width, *refs):
    arrays, messages, sem = refs[:count], refs[-1 - len(groups):-1], refs[-1]
    rows = arrays[0].shape[0]
    slabs = math.gcd(rows // 16, 4) if rows % 16 == 0 else 1
    for m, group in enumerate(groups):
        for i in range(count):
            for j in range(slabs):
                slab = pl.ds(j * (rows // slabs), rows // slabs)
                pltpu.make_async_copy(
                    arrays[i].at[slab, columns(group, span, base, width)],
                    messages[m].at[i, slab],
                    sem.at[m],
                ).start()
    for m in range(len(groups)):
        pltpu.make_async_copy(messages[m], messages[m], sem.at[m]).wait()


def pack(arrays, groups, span, base, width, after=()):
    count = len(arrays)
    rows = arrays[0].shape[0]
    message = pltpu.VMEM((count, rows, width), arrays[0].dtype)
    size = len(groups) * count * rows * width * 2
    return pl.pallas_call(
        functools.partial(pack_kernel, groups, count, span, base, width),
        out_shape=[message] * len(groups),
        in_specs=[FAR] * count + [ANYWHERE] * len(after),
        out_specs=[WHOLE] * len(groups),
        scratch_shapes=[pltpu.SemaphoreType.DMA((len(groups),))],
        compiler_params=limit(size),
        cost_estimate=pl.CostEstimate(flops=0, bytes_accessed=2 * size, transcendentals=0),
        name="pack",
    )(*(pltpu.with_memory_space_constraint(array, pltpu.HBM) for array in arrays), *after)


def place_kernel(groups, span, base, width, *refs):
    count = len(groups)
    messages, outs, sems = refs[:count], refs[-3:-1], refs[-1]
    run(
        [
            pltpu.make_async_copy(
                messages[m].at[i],
                outs[i].at[:, columns(group, span, base, width)],
                sems.at[m, i],
            )
            for m, group in enumerate(groups)
            for i in range(2)
        ]
    )


def place(outs, messages, groups, span, base, shape):
    count = len(messages)
    _, rows, width = messages[0].shape
    out = jax.ShapeDtypeStruct(shape, messages[0].dtype)
    return pl.pallas_call(
        functools.partial(place_kernel, groups, span, base, width),
        out_shape=[out, out],
        in_specs=[WHOLE] * count + [FAR] * len(outs),
        out_specs=[FAR, FAR],
        scratch_shapes=[pltpu.SemaphoreType.DMA((count, 2))],
        input_output_aliases={count + i: i for i in range(len(outs))},
        compiler_params=limit(count * rows * width * 4),
        cost_estimate=pl.CostEstimate(
            flops=0, bytes_accessed=count * rows * width * 8, transcendentals=0
        ),
        name="place",
    )(*messages, *outs)


def attend_kernel(layout, *refs):
    messages = []
    for counts in layout:
        parts, refs = refs[:len(counts)], refs[len(counts):]
        messages.append([part.at[i] for part, count in zip(parts, counts) for i in range(count)])
    results = refs

    def joined(which):
        return jnp.concatenate([message[which][...] for message in messages], axis=0)

    keys = joined(1)
    values = joined(2)
    both_keys = jnp.concatenate([keys, joined(4)], axis=1)
    both_values = jnp.concatenate([values, joined(5)], axis=1)
    width = keys.shape[1]
    scale = width ** -0.5
    across = (((1,), (1,)), ((), ()))
    for message, result in zip(messages, results):
        queries = message[0][...]
        paired = jnp.concatenate([message[3][...], queries], axis=1)
        scores = lax.dot_general(queries, keys, across, preferred_element_type=jnp.float32)
        tangent = lax.dot_general(paired, both_keys, across, preferred_element_type=jnp.float32)
        row_max = jnp.max(scores, axis=1, keepdims=True)
        raised = jnp.exp2((scores - row_max) * (scale * math.log2(math.e)))
        exact = raised * (1.0 / jnp.sum(raised, axis=1, keepdims=True))
        weights = exact.astype(jnp.bfloat16)
        mean = jnp.sum(exact * tangent, axis=1, keepdims=True)
        weight_tangent = (exact * ((tangent - mean) * scale)).astype(jnp.bfloat16)
        sums = jnp.dot(weights, both_values, preferred_element_type=jnp.float32)
        moved = jnp.dot(weight_tangent, values, preferred_element_type=jnp.float32)
        result[0] = sums[:, :width].astype(jnp.bfloat16)
        result[1] = (sums[:, width:] + moved).astype(jnp.bfloat16)


def attend(messages):
    groups = len(messages)
    parts = [part for message in messages for part in message]
    layout = [[part.shape[0] for part in message] for message in messages]
    _, rows, width = parts[0].shape
    heads = width // HEAD
    tokens = rows * groups
    return pl.pallas_call(
        functools.partial(attend_kernel, layout),
        out_shape=[jax.ShapeDtypeStruct((2, rows, width), jnp.bfloat16)] * groups,
        grid=(heads,),
        in_specs=[
            pl.BlockSpec((part.shape[0], rows, HEAD), lambda h: (0, 0, h)) for part in parts
        ],
        out_specs=[pl.BlockSpec((2, rows, HEAD), lambda h: (0, 0, h))] * groups,
        compiler_params=limit(32 * tokens * HEAD * 2, 32 * rows * tokens * 4),
        cost_estimate=pl.CostEstimate(
            flops=heads * 12 * tokens * tokens * HEAD,
            bytes_accessed=heads * 16 * tokens * HEAD,
            transcendentals=heads * tokens * tokens,
        ),
        name="attend",
    )(*parts)


def on_device(*arrays):
    count = lax.axis_size("seq")
    shape = arrays[0].shape
    span = shape[1] // count
    rounds = rounds_of(count)
    groups = [group for group, _ in rounds]

    def there(message, r):
        return lax.ppermute(message, "seq", list(enumerate(rounds[r][1])))

    def back(message, r):
        return lax.ppermute(message, "seq", [(b, a) for a, b in enumerate(rounds[r][1])])

    chunks = []
    base = 0
    for heads in chunk_sizes(span // HEAD):
        chunks.append((base, heads * HEAD))
        base += heads * HEAD
    received = []
    for base, width in chunks:
        parts = [arrays[:2], arrays[2:4], arrays[4:]] if base == 0 else [arrays]
        sent = [[*(pack(part, [group], span, base, width)[0] for part in parts)] for group in groups]
        own = pack(arrays, [own_group], span, base, width, after=sent[-1])
        received.append([own, *([there(part, r) for part in m] for r, m in enumerate(sent))])
    outs = ()
    for (base, width), messages in zip(chunks, received):
        own, *results = attend(messages)
        returned = [back(m, r) for r, m in enumerate(results)]
        outs = place(outs, [own], [own_group], span, base, shape)
        for group, message in zip(groups, returned):
            outs = place(outs, [message], [group], span, base, shape)
    return tuple(outs)


def solution(mesh):
    spec = P(("dp", "seq"), None)
    return jax.shard_map(
        on_device, mesh=mesh, in_specs=(spec,) * 6, out_specs=(spec, spec), check_vma=False
    )
```

```python
import functools
import math

import jax
import jax.numpy as jnp
from jax import lax
from jax.experimental import pallas as pl
from jax.experimental.pallas import tpu as pltpu
from jax.sharding import PartitionSpec as P

HEAD = 128
ANYWHERE = pl.BlockSpec(memory_space=pl.ANY)
FAR = pl.BlockSpec(memory_space=pltpu.HBM)
WHOLE = pl.BlockSpec(memory_space=pltpu.VMEM)


def limit(*sizes):
    return pltpu.CompilerParams(vmem_limit_bytes=sum(sizes) + 2**20)


def chunk_sizes(count):
    last = max(1, 3 * count // 8)
    return [count - last, last] if count > 1 else [count]


def rounds_of(count):
    if count & (count - 1) == 0 and count > 2:
        half = count // 2

        def partner(step, me):
            return me ^ step if step < half else me ^ step ^ lax.div(me, half)

        def static(step, i):
            return i ^ step if step < half else i ^ step ^ (i // half)

        return [
            (functools.partial(partner, step), [static(step, i) for i in range(count)])
            for step in range(1, count)
        ]
    return [
        (lambda me, step=step: lax.rem(me + step, count), [(i + step) % count for i in range(count)])
        for step in range(1, count)
    ]


def own_group(me):
    return me


def columns(group, span, base, width):
    start = group(lax.axis_index("seq")) * span + base
    return pl.ds(pl.multiple_of(start, HEAD), width)


def run(copies):
    for copy in copies:
        copy.start()
    for copy in copies:
        copy.wait()


def pack_kernel(groups, count, span, base, width, *refs):
    arrays, messages, sems = refs[:count], refs[-1 - len(groups):-1], refs[-1]
    run(
        [
            pltpu.make_async_copy(
                arrays[i].at[:, columns(group, span, base, width)],
                messages[m].at[i],
                sems.at[m, i],
            )
            for m, group in enumerate(groups)
            for i in range(count)
        ]
    )


def pack(arrays, groups, span, base, width, after=()):
    count = len(arrays)
    rows = arrays[0].shape[0]
    message = pltpu.VMEM((count, rows, width), arrays[0].dtype)
    size = len(groups) * count * rows * width * 2
    return pl.pallas_call(
        functools.partial(pack_kernel, groups, count, span, base, width),
        out_shape=[message] * len(groups),
        in_specs=[FAR] * count + [ANYWHERE] * len(after),
        out_specs=[WHOLE] * len(groups),
        scratch_shapes=[pltpu.SemaphoreType.DMA((len(groups), count))],
        compiler_params=limit(size),
        cost_estimate=pl.CostEstimate(flops=0, bytes_accessed=2 * size, transcendentals=0),
        name="pack",
    )(*(pltpu.with_memory_space_constraint(array, pltpu.HBM) for array in arrays), *after)


def place_kernel(groups, span, base, width, *refs):
    count = len(groups)
    messages, outs, sems = refs[:count], refs[-3:-1], refs[-1]
    run(
        [
            pltpu.make_async_copy(
                messages[m].at[i],
                outs[i].at[:, columns(group, span, base, width)],
                sems.at[m, i],
            )
            for m, group in enumerate(groups)
            for i in range(2)
        ]
    )


def place(outs, messages, groups, span, base, shape):
    count = len(messages)
    _, rows, width = messages[0].shape
    out = jax.ShapeDtypeStruct(shape, messages[0].dtype)
    return pl.pallas_call(
        functools.partial(place_kernel, groups, span, base, width),
        out_shape=[out, out],
        in_specs=[WHOLE] * count + [FAR] * len(outs),
        out_specs=[FAR, FAR],
        scratch_shapes=[pltpu.SemaphoreType.DMA((count, 2))],
        input_output_aliases={count + i: i for i in range(len(outs))},
        compiler_params=limit(count * rows * width * 4),
        cost_estimate=pl.CostEstimate(
            flops=0, bytes_accessed=count * rows * width * 8, transcendentals=0
        ),
        name="place",
    )(*messages, *outs)


def attend_kernel(layout, *refs):
    messages = []
    for counts in layout:
        parts, refs = refs[:len(counts)], refs[len(counts):]
        messages.append([part.at[i] for part, count in zip(parts, counts) for i in range(count)])
    results = refs

    def joined(which):
        return jnp.concatenate([message[which][...] for message in messages], axis=0)

    keys = joined(1)
    values = joined(2)
    both_keys = jnp.concatenate([keys, joined(4)], axis=1)
    both_values = jnp.concatenate([values, joined(5)], axis=1)
    width = keys.shape[1]
    scale = width ** -0.5
    across = (((1,), (1,)), ((), ()))
    for message, result in zip(messages, results):
        queries = message[0][...]
        paired = jnp.concatenate([message[3][...], queries], axis=1)
        scores = lax.dot_general(queries, keys, across, preferred_element_type=jnp.float32)
        tangent = lax.dot_general(paired, both_keys, across, preferred_element_type=jnp.float32)
        row_max = jnp.max(scores, axis=1, keepdims=True)
        raised = jnp.exp2((scores - row_max) * (scale * math.log2(math.e)))
        exact = raised * (1.0 / jnp.sum(raised, axis=1, keepdims=True))
        weights = exact.astype(jnp.bfloat16)
        mean = jnp.sum(exact * tangent, axis=1, keepdims=True)
        weight_tangent = (exact * ((tangent - mean) * scale)).astype(jnp.bfloat16)
        sums = jnp.dot(weights, both_values, preferred_element_type=jnp.float32)
        moved = jnp.dot(weight_tangent, values, preferred_element_type=jnp.float32)
        result[0] = sums[:, :width].astype(jnp.bfloat16)
        result[1] = (sums[:, width:] + moved).astype(jnp.bfloat16)


def attend(messages):
    groups = len(messages)
    parts = [part for message in messages for part in message]
    layout = [[part.shape[0] for part in message] for message in messages]
    _, rows, width = parts[0].shape
    heads = width // HEAD
    tokens = rows * groups
    return pl.pallas_call(
        functools.partial(attend_kernel, layout),
        out_shape=[jax.ShapeDtypeStruct((2, rows, width), jnp.bfloat16)] * groups,
        grid=(heads,),
        in_specs=[
            pl.BlockSpec((part.shape[0], rows, HEAD), lambda h: (0, 0, h)) for part in parts
        ],
        out_specs=[pl.BlockSpec((2, rows, HEAD), lambda h: (0, 0, h))] * groups,
        compiler_params=limit(32 * tokens * HEAD * 2, 32 * rows * tokens * 4),
        cost_estimate=pl.CostEstimate(
            flops=heads * 12 * tokens * tokens * HEAD,
            bytes_accessed=heads * 16 * tokens * HEAD,
            transcendentals=heads * tokens * tokens,
        ),
        name="attend",
    )(*parts)


def on_device(*arrays):
    count = lax.axis_size("seq")
    shape = arrays[0].shape
    span = shape[1] // count
    rounds = rounds_of(count)
    groups = [group for group, _ in rounds]

    def there(message, r):
        return lax.ppermute(message, "seq", list(enumerate(rounds[r][1])))

    def back(message, r):
        return lax.ppermute(message, "seq", [(b, a) for a, b in enumerate(rounds[r][1])])

    chunks = []
    base = 0
    for heads in chunk_sizes(span // HEAD):
        chunks.append((base, heads * HEAD))
        base += heads * HEAD
    received = []
    for base, width in chunks:
        sent = [pack(arrays, [group], span, base, width) for group in groups]
        own = pack(arrays, [own_group], span, base, width, after=sent[-1])
        received.append([own, *([there(part, r) for part in m] for r, m in enumerate(sent))])
    outs = ()
    for (base, width), messages in zip(chunks, received):
        own, *results = attend(messages)
        order = range(len(groups)) if base else reversed(range(len(groups)))
        sends = {r: back(results[r], r) for r in order}
        returned = [sends[r] for r in range(len(groups))]
        outs = place(outs, [own], [own_group], span, base, shape)
        for group, message in zip(groups, returned):
            outs = place(outs, [message], [group], span, base, shape)
    return tuple(outs)


def solution(mesh):
    spec = P(("dp", "seq"), None)
    return jax.shard_map(
        on_device, mesh=mesh, in_specs=(spec,) * 6, out_specs=(spec, spec), check_vma=False
    )
```
